32 devices in a mesh: gx: 8 (over z, x), gy: 4 (over y, core).
Axes of the slice: x: 2, y: 2, z: 4, core: 2. Of those that a mesh axis runs over, the one named last changes fastest.
Arguments:
- volume: float32 [64, 16, 32, 128], P(None, 'gx', 'gy'), may hold values from -6 to 6
- cotangent: float32 [64, 16, 32, 128], P(None, 'gx', 'gy'), may hold values from -20 to 20
- weight_one: float32 [27, 4096], replicated, may hold values from -0.17 to 0.16, as said below
- scale_one: float32 [64], replicated, may hold values from 0.001 to 0.016
- weight_two: float32 [27, 4096], replicated, may hold values from -0.17 to 0.16, as said below
- scale_two: float32 [64], replicated, may hold values from 0.001 to 0.016
Outputs:
- input_grad: float32 [64, 16, 32, 128], P(None, 'gx', 'gy')
- kernel_grad_one: float32 [27, 4096], P(None, ('gx', 'gy'))
- scale_grad_one: float32 [64], replicated
- kernel_grad_two: float32 [27, 4096], P(None, ('gx', 'gy'))
- scale_grad_two: float32 [64], replicated
The draws below stay inside these ranges and needn't reach their ends.
Inputs may be any that keep to these rules, and one draw needn't show every extreme that they name: `weight_one`: each entry divided by its output channel's entry of scale_one lies 0.1 to 0.4 away from the nearest integer, between -10.4 and 9.4. `weight_two`: each entry divided by its output channel's entry of scale_two lies 0.1 to 0.4 away from the nearest integer, between -10.4 and 9.4.
All inputs are finite; a program needn't handle non-finite values.
Results may differ from the reference program's by a relative error of at most 0.0003.
Values sent between devices are 32-bit elements; how exact they have to be, the bound alone decides.
A program may use at most 128 MiB of HBM per device.

```python
import jax
import jax.numpy as jnp
from jax import lax

CH = 64
ZW = 128
NX = 16
NY = 32


def lsq_pair(key, salt):
    base = jax.random.fold_in(key, salt)
    key_scale, key_level, key_frac, key_sign = jax.random.split(base, 4)
    lowest, highest = (0.002, 0.008)
    scales = jnp.exp(jax.random.uniform(key_scale, (CH,), jnp.float32, jnp.log(lowest), jnp.log(highest)))
    levels = jax.random.randint(key_level, (27, CH, CH), -10, 10).astype(jnp.float32)
    fraction = jax.random.uniform(key_frac, (27, CH, CH), jnp.float32, 0.1, 0.4)
    signs = jnp.where(jax.random.bernoulli(key_sign, 0.5, (27, CH, CH)), 1.0, -1.0)
    weight = scales[None, :, None] * (levels + signs * fraction)
    return (weight.reshape(27, CH * CH), scales)


def draw_weight_one(key, part):
    return lsq_pair(key, 11)[0]


def draw_scale_one(key, part):
    return lsq_pair(key, 11)[1]


def draw_weight_two(key, part):
    return lsq_pair(key, 23)[0]


def draw_scale_two(key, part):
    return lsq_pair(key, 23)[1]


def draw_cotangent(key, part):
    key_noise = jax.random.fold_in(jax.random.fold_in(key, 37), 0)
    noise = jax.random.truncated_normal(key_noise, -4.0, 4.0, (CH, NX, NY, ZW), jnp.float32)
    along_x = jnp.arange(NX, dtype=jnp.float32) / max(NX - 1, 1)
    along_y = jnp.arange(NY, dtype=jnp.float32) / max(NY - 1, 1)
    ramp = (along_x[:, None] + along_y[None, :]) / 2.0
    amplitude = 0.6 * 3.0 ** ramp
    return noise * amplitude[None, :, :, None]


def block_levels(key, dims, shards, smallest, top_value):
    def one(dim, shards_of):
        heights = jax.random.uniform(jax.random.fold_in(jax.random.fold_in(key, 6), dim), (shards_of,), jnp.float32, smallest / len(shards), top_value / len(shards))
        return jnp.repeat(jnp.exp(heights), dims[dim] // shards_of).reshape((-1,) + (1,) * (len(dims) - dim - 1))

    level = one(*shards[0])
    for cut in shards[1:]:
        level = level * one(*cut)
    return level


def centred(rng, shape, scale, bound, pieces=(), held_as=jnp.bfloat16):
    array = scale * jax.random.normal(rng, shape, jnp.float32)
    if pieces:
        array = array * block_levels(rng, shape, pieces, -0.22, 0.18)
    return jnp.clip(array, -bound, bound).astype(held_as)


def setup_inputs(seed: int = 0) -> dict:
    seeds = jax.random.split(jax.random.key(seed), 7)
    return {
        "volume": centred(seeds[0], (CH, NX, NY, ZW), 1.0, 6.0, ((1, 8), (2, 4)), jnp.float32),
        "cotangent": draw_cotangent(jax.random.fold_in(seeds[6], 71), 0),
        "weight_one": draw_weight_one(jax.random.fold_in(seeds[6], 71), 0),
        "scale_one": draw_scale_one(jax.random.fold_in(seeds[6], 71), 0),
        "weight_two": draw_weight_two(jax.random.fold_in(seeds[6], 71), 0),
        "scale_two": draw_scale_two(jax.random.fold_in(seeds[6], 71), 0),
    }


CODE_LOW = -8.0
CODE_HIGH = 7.0
REPORT = 2.0 ** (-10)

def quantize(weight, scales):
    channels = scales.shape[0]
    ratios = weight.reshape(27, channels, channels) / scales[None, :, None]
    levels = jnp.clip(jnp.floor(ratios + 0.5), CODE_LOW, CODE_HIGH)
    inside = jnp.logical_and(ratios >= CODE_LOW, ratios <= CODE_HIGH)
    residue = jnp.where(inside, levels - ratios, levels)
    return (levels * scales[None, :, None], inside, residue)

def to_kernel(tap_weights):
    channels = tap_weights.shape[1]
    return tap_weights.reshape(3, 3, 3, channels, channels).transpose(3, 4, 0, 1, 2)

def convolve(signal, kernel):
    return lax.conv_general_dilated(signal[None], kernel, (1, 1, 1), ((1, 1), (1, 1), (1, 1)), dimension_numbers=('NCDHW', 'OIDHW', 'NCDHW'), precision=lax.Precision.HIGHEST)[0]

def forward(signal, taps_first, taps_second):
    hidden = jax.nn.silu(convolve(signal, to_kernel(taps_first)))
    return jax.nn.silu(convolve(hidden, to_kernel(taps_second)))

def reference(volume, cotangent, weight_one, scale_one, weight_two, scale_two):
    taps_one, inside_one, residue_one = quantize(weight_one, scale_one)
    taps_two, inside_two, residue_two = quantize(weight_two, scale_two)
    outcome, pullback = jax.vjp(forward, volume, taps_one, taps_two)
    input_grad, grad_one, grad_two = pullback(cotangent)
    factor = REPORT * (27.0 * CH * CODE_HIGH) ** (-0.5)
    kernel_grad_one = (jnp.where(inside_one, grad_one, 0.0) * REPORT).reshape(27, CH * CH)
    kernel_grad_two = (jnp.where(inside_two, grad_two, 0.0) * REPORT).reshape(27, CH * CH)
    scale_grad_one = factor * lax.optimization_barrier(jnp.sum(grad_one * residue_one, axis=(0, 2)))
    scale_grad_two = factor * lax.optimization_barrier(jnp.sum(grad_two * residue_two, axis=(0, 2)))
    return (input_grad, kernel_grad_one, scale_grad_one, kernel_grad_two, scale_grad_two)
```

```python
import functools

import jax
import jax.numpy as jnp
from jax import lax
from jax.experimental import pallas as pl
from jax.experimental.pallas import tpu as pltpu
from jax.sharding import PartitionSpec as P

CODE_LOW = -8.0
CODE_HIGH = 7.0
REPORT = 2.0 ** (-10)
WAYS = [(dx, dy) for dx in (-1, 0, 1) for dy in (-1, 0, 1) if (dx, dy) != (0, 0)]


def quantize(weight, scales):
    channels = scales.shape[0]
    ratios = weight.reshape(27, channels, channels) / scales[None, :, None]
    levels = jnp.clip(jnp.floor(ratios + 0.5), CODE_LOW, CODE_HIGH)
    inside = jnp.logical_and(ratios >= CODE_LOW, ratios <= CODE_HIGH)
    residue = jnp.where(inside, levels - ratios, levels)
    return (levels, inside, residue)


def forward_matrix(levels):
    ch = levels.shape[1]
    taps = levels.astype(jnp.bfloat16).reshape(3, 3, 3, ch, ch).transpose(0, 2, 3, 1, 4)
    taps = jnp.broadcast_to(taps[:, :, :, :, None, :], (3, 3, ch, 3, 2, ch))
    return taps.reshape(3, 3 * ch, 6 * ch)


def backward_matrix(levels):
    ch = levels.shape[1]
    taps = jnp.flip(levels.astype(jnp.bfloat16).reshape(3, 3, 3, ch, ch), (0, 1, 2))
    taps = taps.transpose(0, 2, 4, 1, 3)
    taps = jnp.broadcast_to(taps[:, :, :, :, None, :], (3, 3, ch, 3, 2, ch))
    return taps.reshape(3, 3 * ch, 6 * ch)


def halves(value):
    high = value.astype(jnp.bfloat16)
    low = (value - high.astype(jnp.float32)).astype(jnp.bfloat16)
    return high, low


def kernel(
    sizes, vol, cot, s1, s2, f1, f2, b2, b1, out, g1, g2,
    pad0, pad1, pad2, pad3, vol_h, hid_h, del_h, stage, slope, send_sem, recv_sem,
):
    nx, ny, ch, width = vol.shape
    size_x, size_y = sizes
    me_x, me_y = lax.axis_index("gx"), lax.axis_index("gy")
    rows = nx * ny
    lane = lax.broadcasted_iota(jnp.int32, (ch, width), 1)

    for pad in (pad0, pad1, pad2, pad3):
        pad[...] = jnp.zeros_like(pad)
    g1[...] = jnp.zeros_like(g1)
    g2[...] = jnp.zeros_like(g2)

    def there(dx, dy):
        x, y = me_x + dx, me_y + dy
        return (x >= 0) & (x < size_x) & (y >= 0) & (y < size_y)

    barrier = pltpu.get_barrier_semaphore()
    count = jnp.int32(0)
    for dx, dy in WAYS:
        valid = there(dx, dy)
        count = count + jnp.where(valid, 1, 0)

        @pl.when(valid)
        def _(dx=dx, dy=dy):
            pl.semaphore_signal(
                barrier, inc=1, device_id=(me_x + dx, me_y + dy),
                device_id_type=pl.DeviceIdType.MESH,
            )

    pl.semaphore_wait(barrier, count)

    def spans(step, length):
        if step == 1:
            return pl.ds(length, 1), pl.ds(0, 1)
        if step == -1:
            return pl.ds(1, 1), pl.ds(length + 1, 1)
        return pl.ds(1, length), pl.ds(1, length)

    def remote(pad, turn, way, dx, dy):
        from_x, to_x = spans(dx, nx)
        from_y, to_y = spans(dy, ny)
        return pltpu.make_async_remote_copy(
            src_ref=pad.at[from_x, from_y],
            dst_ref=pad.at[to_x, to_y],
            send_sem=send_sem.at[turn, way],
            recv_sem=recv_sem.at[turn, way],
            device_id=(me_x + dx, me_y + dy),
            device_id_type=pl.DeviceIdType.MESH,
        )

    def send(pad, turn):
        for way, (dx, dy) in enumerate(WAYS):
            @pl.when(there(dx, dy))
            def _(way=way, dx=dx, dy=dy):
                remote(pad, turn, way, dx, dy).start()

    def receive(pad, turn):
        for way, (dx, dy) in enumerate(WAYS):
            @pl.when(there(-dx, -dy))
            def _(way=way, dx=dx, dy=dy):
                remote(pad, turn, way, dx, dy).wait_recv()

    def sent(pad, turn):
        for way, (dx, dy) in enumerate(WAYS):
            @pl.when(there(dx, dy))
            def _(way=way, dx=dx, dy=dy):
                remote(pad, turn, way, dx, dy).wait_send()

    def split(pad, target):
        for x in range(nx + 2):
            def body(y, carry, x=x):
                high, low = halves(pad[x, y])
                target[x, y, 0:ch, :] = high
                target[x, y, ch:2 * ch, :] = low
                return carry

            lax.fori_loop(0, ny + 2, body, 0)

    def conv_row(source, matrix, x, y):
        total = None
        for a in range(3):
            block = source[x + a, pl.ds(y, 3)].reshape(6 * ch, width)
            part = jnp.dot(matrix[a], block, preferred_element_type=jnp.float32)
            total = part if total is None else total + part
        before = jnp.where(lane == 0, 0.0, pltpu.roll(total[0:ch], 1, 1))
        after = jnp.where(lane == width - 1, 0.0, pltpu.roll(total[2 * ch:3 * ch], width - 1, 1))
        return before + total[ch:2 * ch] + after

    def grad_row(delta, source, target, x, y):
        left = jnp.where(lane == width - 1, 0.0, pltpu.roll(delta, width - 1, 1))
        right = jnp.where(lane == 0, 0.0, pltpu.roll(delta, 1, 1))
        parts = []
        for shifted in (left, delta, right):
            parts.extend(halves(shifted))
        stack = jnp.concatenate(parts, axis=0)
        for a in range(3):
            block = source[x + a, pl.ds(y, 3)].reshape(6 * ch, width)
            prod = lax.dot_general(
                stack, block, (((1,), (1,)), ((), ())), preferred_element_type=jnp.float32
            )
            for c in range(3):
                first = prod[2 * c * ch:(2 * c + 1) * ch]
                second = prod[(2 * c + 1) * ch:(2 * c + 2) * ch]
                target[a, c * ch:(c + 1) * ch, :] += first + second

    def each_row(body):
        for x in range(nx):
            def step(y, carry, x=x):
                body(x, y)
                return carry

            lax.fori_loop(0, ny, step, 0)

    pad0[1:nx + 1, 1:ny + 1] = vol[...]
    send(pad0, 0)
    receive(pad0, 0)
    split(pad0, vol_h)

    def first(x, y):
        pre = conv_row(vol_h, f1, x, y) * s1[...]
        sig = 1.0 / (1.0 + jnp.exp(-pre))
        stage[x, y] = pre * sig
        slope[x, y] = sig * (1.0 + pre * (1.0 - sig))

    each_row(first)

    pad1[1:nx + 1, 1:ny + 1] = stage[...]
    send(pad1, 1)
    receive(pad1, 1)
    split(pad1, hid_h)

    def second(x, y):
        pre = conv_row(hid_h, f2, x, y) * s2[...]
        sig = 1.0 / (1.0 + jnp.exp(-pre))
        stage[x, y] = cot[x, y] * (sig * (1.0 + pre * (1.0 - sig)))

    each_row(second)

    pad2[1:nx + 1, 1:ny + 1] = stage[...] * s2[...]
    send(pad2, 2)
    each_row(lambda x, y: grad_row(stage[x, y], hid_h, g2, x, y))
    receive(pad2, 2)
    split(pad2, del_h)

    def third(x, y):
        stage[x, y] = conv_row(del_h, b2, x, y) * slope[x, y]

    each_row(third)

    pad3[1:nx + 1, 1:ny + 1] = stage[...] * s1[...]
    send(pad3, 3)
    each_row(lambda x, y: grad_row(stage[x, y], vol_h, g1, x, y))
    receive(pad3, 3)
    split(pad3, del_h)

    def fourth(x, y):
        out[x, y] = conv_row(del_h, b1, x, y)

    each_row(fourth)
    for turn, pad in enumerate((pad0, pad1, pad2, pad3)):
        sent(pad, turn)


def gradient(raw, channels):
    taps = raw.reshape(3, 3, channels, 3, 2, channels).sum(axis=4)
    return taps.transpose(0, 3, 1, 2, 4).reshape(27, channels, channels)


def on_device(volume, cotangent, weight_one, scale_one, weight_two, scale_two):
    channels = scale_one.shape[0]
    ch, nx, ny, width = volume.shape
    sizes = (lax.axis_size("gx"), lax.axis_size("gy"))
    level_one, inside_one, residue_one = quantize(weight_one, scale_one)
    level_two, inside_two, residue_two = quantize(weight_two, scale_two)
    vmem = pl.BlockSpec(memory_space=pltpu.VMEM)
    cells = jax.ShapeDtypeStruct((nx, ny, ch, width), jnp.float32)
    grads = jax.ShapeDtypeStruct((3, 3 * ch, 6 * ch), jnp.float32)
    pad = pltpu.VMEM((nx + 2, ny + 2, ch, width), jnp.float32)
    half = pltpu.VMEM((nx + 2, ny + 2, 2 * ch, width), jnp.bfloat16)
    local = pltpu.VMEM((nx, ny, ch, width), jnp.float32)
    moved, raw_one, raw_two = pl.pallas_call(
        functools.partial(kernel, sizes),
        out_shape=(cells, grads, grads),
        in_specs=[vmem] * 8,
        out_specs=(vmem, vmem, vmem),
        scratch_shapes=[
            pad, pad, pad, pad, half, half, half, local, local,
            pltpu.SemaphoreType.DMA((4, 8)),
            pltpu.SemaphoreType.DMA((4, 8)),
        ],
        compiler_params=pltpu.CompilerParams(
            collective_id=0, has_side_effects=True, vmem_limit_bytes=48 * 2 ** 20
        ),
    )(
        volume.transpose(1, 2, 0, 3),
        cotangent.transpose(1, 2, 0, 3),
        jnp.broadcast_to(scale_one[:, None], (ch, width)),
        jnp.broadcast_to(scale_two[:, None], (ch, width)),
        forward_matrix(level_one),
        forward_matrix(level_two),
        backward_matrix(level_two),
        backward_matrix(level_one),
    )
    input_grad = moved.transpose(2, 0, 1, 3)
    devices = sizes[0] * sizes[1]
    share = channels * channels // devices
    factor = REPORT * (27.0 * channels * CODE_HIGH) ** (-0.5)

    grad_one = gradient(raw_one, channels)
    grad_two = gradient(raw_two, channels)
    part_one = jnp.sum(grad_one * residue_one, axis=(0, 2))
    part_two = jnp.sum(grad_two * residue_two, axis=(0, 2))
    kept_one = jnp.where(inside_one, grad_one, 0.0).reshape(27, devices, share)
    kept_two = jnp.where(inside_two, grad_two, 0.0).reshape(27, devices, share)
    both = jnp.concatenate([kept_one, kept_two], axis=0).transpose(1, 0, 2)
    both = both.reshape(devices, 54 * share)
    parts = jnp.broadcast_to(
        jnp.concatenate([part_one, part_two])[None], (devices, 2 * channels)
    )
    blocks = jnp.concatenate([both, parts], axis=1)
    blocks = lax.all_to_all(blocks, ("gx", "gy"), 0, 0, tiled=True)
    total = jnp.sum(blocks, axis=0)
    kernels = total[:54 * share].reshape(2, 27, share) * REPORT
    scales = total[54 * share:].reshape(2, channels) * factor
    return (input_grad, kernels[0], scales[0], kernels[1], scales[1])


def solution(mesh):
    in_specs = (P(None, "gx", "gy", None), P(None, "gx", "gy", None), P(), P(), P(), P())
    out_specs = (P(None, "gx", "gy", None), P(None, ("gx", "gy")), P(), P(None, ("gx", "gy")), P())
    return jax.shard_map(
        on_device, mesh=mesh, in_specs=in_specs, out_specs=out_specs, check_vma=False
    )
```

```python
import functools

import jax
import jax.numpy as jnp
from jax import lax
from jax.experimental import pallas as pl
from jax.experimental.pallas import tpu as pltpu
from jax.sharding import PartitionSpec as P

CODE_LOW = -8.0
CODE_HIGH = 7.0
REPORT = 2.0 ** (-10)
WAYS = [(dx, dy) for dx in (-1, 0, 1) for dy in (-1, 0, 1) if (dx, dy) != (0, 0)]


def quantize(weight, scale):
    ratio = weight / scale
    level = jnp.clip(jnp.floor(ratio + 0.5), CODE_LOW, CODE_HIGH)
    inside = jnp.logical_and(ratio >= CODE_LOW, ratio <= CODE_HIGH)
    return level, inside, jnp.where(inside, level - ratio, level)


def halves(value):
    high = value.astype(jnp.bfloat16)
    low = (value - high.astype(jnp.float32)).astype(jnp.bfloat16)
    return high, low


def kernel(
    sizes, vol, cot, s1, s2, w1, w2, out, share1, share2,
    pad0, pad1, pad2, pad3, vol_h, hid_h, del_h, stage, slope,
    f1, f2, b2, b1, g1, g2, folded, box1, box2, land1, land2,
    send_sem, recv_sem, out_sem, in_sem,
):
    nx, ny, ch, width = vol.shape
    size_x, size_y = sizes
    me_x, me_y = lax.axis_index("gx"), lax.axis_index("gy")
    devices = size_x * size_y
    me = me_x * size_y + me_y
    group = devices // box1.shape[0]
    lane = lax.broadcasted_iota(jnp.int32, (ch, width), 1)

    for pad in (pad0, pad1, pad2, pad3):
        pad[...] = jnp.zeros_like(pad)

    def there(dx, dy):
        x, y = me_x + dx, me_y + dy
        return (x >= 0) & (x < size_x) & (y >= 0) & (y < size_y)

    barrier = pltpu.get_barrier_semaphore()

    def greet(k, carry):
        other = lax.rem(me + k, devices)
        pl.semaphore_signal(
            barrier, inc=1, device_id=(other // size_y, lax.rem(other, size_y)),
            device_id_type=pl.DeviceIdType.MESH,
        )
        return carry

    lax.fori_loop(1, devices, greet, 0)
    pad0[1:nx + 1, 1:ny + 1] = vol[...]
    pl.semaphore_wait(barrier, devices - 1)

    def spans(step, length):
        if step == 1:
            return pl.ds(length, 1), pl.ds(0, 1)
        if step == -1:
            return pl.ds(1, 1), pl.ds(length + 1, 1)
        return pl.ds(1, length), pl.ds(1, length)

    def remote(pad, turn, way, dx, dy):
        from_x, to_x = spans(dx, nx)
        from_y, to_y = spans(dy, ny)
        return pltpu.make_async_remote_copy(
            src_ref=pad.at[from_x, from_y],
            dst_ref=pad.at[to_x, to_y],
            send_sem=send_sem.at[turn, way],
            recv_sem=recv_sem.at[turn, way],
            device_id=(me_x + dx, me_y + dy),
            device_id_type=pl.DeviceIdType.MESH,
        )

    def send(pad, turn):
        for way, (dx, dy) in enumerate(WAYS):
            @pl.when(there(dx, dy))
            def _(way=way, dx=dx, dy=dy):
                remote(pad, turn, way, dx, dy).start()

    def receive(pad, turn):
        for way, (dx, dy) in enumerate(WAYS):
            @pl.when(there(-dx, -dy))
            def _(way=way, dx=dx, dy=dy):
                remote(pad, turn, way, dx, dy).wait_recv()

    def sent(pad, turn):
        for way, (dx, dy) in enumerate(WAYS):
            @pl.when(there(dx, dy))
            def _(way=way, dx=dx, dy=dy):
                remote(pad, turn, way, dx, dy).wait_send()

    def split(pad, target):
        for x in range(nx + 2):
            def body(y, carry, x=x):
                high, low = halves(pad[x, y])
                target[x, y, 0:ch, :] = high
                target[x, y, ch:2 * ch, :] = low
                return carry

            lax.fori_loop(0, ny + 2, body, 0)

    def matrices(weight, scale, forward, backward):
        for a in range(3):
            for b in range(3):
                for c in range(3):
                    level, _, _ = quantize(weight[9 * a + 3 * b + c], scale[...])
                    flipped = jnp.concatenate([level, level], axis=0).T[0:ch]
                    at = (3 * a + b) * 2 * ch
                    forward[c * ch:(c + 1) * ch, at:at + 2 * ch] = level.astype(jnp.bfloat16)
                    at = (3 * (2 - a) + 2 - b) * 2 * ch
                    backward[(2 - c) * ch:(3 - c) * ch, at:at + 2 * ch] = flipped.astype(
                        jnp.bfloat16
                    )

    def around(source, x, y):
        blocks = []
        for k in (0, 1):
            blocks.append(jnp.concatenate(
                [source[x + a, pl.ds(y + k, 3)].reshape(6 * ch, width) for a in range(3)],
                axis=0,
            ))
        return jnp.concatenate(blocks, axis=1)

    def conv_rows(source, matrix, x, y):
        total = jnp.dot(
            matrix[...], around(source, x, y), preferred_element_type=jnp.float32
        )
        rows = []
        for k in (0, 1):
            part = total[:, k * width:(k + 1) * width]
            before = jnp.where(lane == 0, 0.0, pltpu.roll(part[0:ch], 1, 1))
            after = jnp.where(
                lane == width - 1, 0.0, pltpu.roll(part[2 * ch:3 * ch], width - 1, 1)
            )
            rows.append(before + part[ch:2 * ch] + after)
        return rows

    def grad_rows(source, target, x, y):
        stacks = []
        for k in (0, 1):
            delta = stage[x, y + k]
            left = jnp.where(lane == width - 1, 0.0, pltpu.roll(delta, width - 1, 1))
            right = jnp.where(lane == 0, 0.0, pltpu.roll(delta, 1, 1))
            parts = []
            for shifted in (left, delta, right):
                parts.extend(halves(shifted))
            stacks.append(jnp.concatenate(parts, axis=0))
        prod = lax.dot_general(
            jnp.concatenate(stacks, axis=1), around(source, x, y),
            (((1,), (1,)), ((), ())), preferred_element_type=jnp.float32,
        )
        for c in range(3):
            first = prod[2 * c * ch:(2 * c + 1) * ch]
            second = prod[(2 * c + 1) * ch:(2 * c + 2) * ch]
            target[c * ch:(c + 1) * ch, :] += first + second

    def each_pair(body):
        for x in range(nx):
            def step(j, carry, x=x):
                body(x, 2 * j)
                return carry

            lax.fori_loop(0, ny // 2, step, 0)

    def collect(target, weight, scale, box):
        summed = jnp.zeros((ch, 2 * ch), jnp.float32)
        for a in range(3):
            for b in range(3):
                for c in range(3):
                    tap = 9 * a + 3 * b + c
                    at = (3 * a + b) * 2 * ch
                    value = target[c * ch:(c + 1) * ch, at:at + 2 * ch]
                    value = value + pltpu.roll(value, ch, 1)
                    _, inside, residue = quantize(weight[tap], scale[...])
                    summed = summed + value * residue
                    folded[tap] = jnp.where(inside, value, 0.0)
        line = 0.5 * jnp.sum(jnp.concatenate([summed, summed], axis=0).T, axis=0, keepdims=True)
        half = lax.broadcasted_iota(jnp.int32, (ch // 2, 2 * ch), 1) < ch
        for tap in range(27):
            even = folded[tap, pl.ds(0, ch // 2, stride=2), :]
            odd = folded[tap, pl.ds(1, ch // 2, stride=2), :]
            box[:, tap, :] = jnp.where(half, even, odd)
        box[:, 27, :] = jnp.broadcast_to(line, (ch // 2, 2 * ch))

    def scatter(box, land, turn):
        def one(k, carry):
            other = lax.rem(me + k, devices)
            pltpu.make_async_remote_copy(
                src_ref=box.at[other // group],
                dst_ref=land.at[k],
                send_sem=out_sem.at[turn],
                recv_sem=in_sem.at[turn],
                device_id=(other // size_y, lax.rem(other, size_y)),
                device_id_type=pl.DeviceIdType.MESH,
            ).start()
            return carry

        lax.fori_loop(1, devices, one, 0)
        land[0] = box[me // group]

    def gather(land, turn, share):
        others = land.at[pl.ds(1, devices - 1)]
        pltpu.make_async_copy(others, others, in_sem.at[turn]).wait()

        def add(source, total):
            return total + land[lax.rem(me - source + devices, devices)]

        share[...] = lax.fori_loop(0, devices, add, jnp.zeros(share.shape, jnp.float32))
        pltpu.make_async_copy(others, others, out_sem.at[turn]).wait()

    send(pad0, 0)
    matrices(w1, s1, f1, b1)
    matrices(w2, s2, f2, b2)
    g1[...] = jnp.zeros_like(g1)
    g2[...] = jnp.zeros_like(g2)
    box1[...] = jnp.zeros_like(box1)
    box2[...] = jnp.zeros_like(box2)
    receive(pad0, 0)
    split(pad0, vol_h)

    def first(x, y):
        for k, row in enumerate(conv_rows(vol_h, f1, x, y)):
            pre = row * s1[...]
            sig = 1.0 / (1.0 + jnp.exp(-pre))
            stage[x, y + k] = pre * sig
            slope[x, y + k] = sig * (1.0 + pre * (1.0 - sig))

    each_pair(first)

    pad1[1:nx + 1, 1:ny + 1] = stage[...]
    send(pad1, 1)
    receive(pad1, 1)
    split(pad1, hid_h)

    def second(x, y):
        for k, row in enumerate(conv_rows(hid_h, f2, x, y)):
            pre = row * s2[...]
            sig = 1.0 / (1.0 + jnp.exp(-pre))
            stage[x, y + k] = cot[x, y + k] * (sig * (1.0 + pre * (1.0 - sig)))

    each_pair(second)

    pad2[1:nx + 1, 1:ny + 1] = stage[...] * s2[...]
    send(pad2, 2)
    each_pair(lambda x, y: grad_rows(hid_h, g2, x, y))
    collect(g2, w2, s2, box2)
    scatter(box2, land2, 1)
    receive(pad2, 2)
    split(pad2, del_h)

    def third(x, y):
        for k, row in enumerate(conv_rows(del_h, b2, x, y)):
            stage[x, y + k] = row * slope[x, y + k]

    each_pair(third)

    pad3[1:nx + 1, 1:ny + 1] = stage[...] * s1[...]
    send(pad3, 3)
    each_pair(lambda x, y: grad_rows(vol_h, g1, x, y))
    collect(g1, w1, s1, box1)
    scatter(box1, land1, 0)
    receive(pad3, 3)
    split(pad3, del_h)

    def fourth(x, y):
        for k, row in enumerate(conv_rows(del_h, b1, x, y)):
            out[x, y + k] = row

    each_pair(fourth)
    gather(land2, 1, share2)
    gather(land1, 0, share1)
    for turn, pad in enumerate((pad0, pad1, pad2, pad3)):
        sent(pad, turn)


def on_device(volume, cotangent, weight_one, scale_one, weight_two, scale_two):
    channels = scale_one.shape[0]
    ch, nx, ny, width = volume.shape
    sizes = (lax.axis_size("gx"), lax.axis_size("gy"))
    devices = sizes[0] * sizes[1]
    vmem = pl.BlockSpec(memory_space=pltpu.VMEM)
    cells = jax.ShapeDtypeStruct((nx, ny, ch, width), jnp.float32)
    block = jax.ShapeDtypeStruct((32, 2 * ch), jnp.float32)
    pad = pltpu.VMEM((nx + 2, ny + 2, ch, width), jnp.float32)
    half = pltpu.VMEM((nx + 2, ny + 2, 2 * ch, width), jnp.bfloat16)
    local = pltpu.VMEM((nx, ny, ch, width), jnp.float32)
    matrix = pltpu.VMEM((3 * ch, 18 * ch), jnp.bfloat16)
    grads = pltpu.VMEM((3 * ch, 18 * ch), jnp.float32)
    box = pltpu.VMEM((ch // 2, 32, 2 * ch), jnp.float32)
    land = pltpu.VMEM((devices, 32, 2 * ch), jnp.float32)

    def twice(weight):
        taps = weight.reshape(27, ch, ch)
        return jnp.concatenate([taps, taps], axis=2)

    moved, block_one, block_two = pl.pallas_call(
        functools.partial(kernel, sizes),
        out_shape=(cells, block, block),
        in_specs=[vmem] * 6,
        out_specs=(vmem, vmem, vmem),
        scratch_shapes=[
            pad, pad, pad, pad, half, half, half, local, local,
            matrix, matrix, matrix, matrix, grads, grads,
            pltpu.VMEM((27, ch, 2 * ch), jnp.float32), box, box, land, land,
            pltpu.SemaphoreType.DMA((4, 8)),
            pltpu.SemaphoreType.DMA((4, 8)),
            pltpu.SemaphoreType.DMA((2,)),
            pltpu.SemaphoreType.DMA((2,)),
        ],
        compiler_params=pltpu.CompilerParams(
            collective_id=0, has_side_effects=True, vmem_limit_bytes=52 * 2 ** 20
        ),
    )(
        volume.transpose(1, 2, 0, 3),
        cotangent.transpose(1, 2, 0, 3),
        jnp.broadcast_to(scale_one[:, None], (ch, width)),
        jnp.broadcast_to(scale_two[:, None], (ch, width)),
        twice(weight_one),
        twice(weight_two),
    )
    input_grad = moved.transpose(2, 0, 1, 3)
    share = channels * channels // devices
    group = 2 * ch // share
    first_col = lax.rem(lax.axis_index(("gx", "gy")), group) * share
    factor = REPORT * (27.0 * channels * CODE_HIGH) ** (-0.5)

    def results(block):
        kernels = lax.dynamic_slice(block, (0, first_col), (27, share)) * REPORT
        return kernels, block[27, :channels] * factor

    kernel_one, scales_one = results(block_one)
    kernel_two, scales_two = results(block_two)
    return (input_grad, kernel_one, scales_one, kernel_two, scales_two)


def solution(mesh):
    in_specs = (P(None, "gx", "gy", None), P(None, "gx", "gy", None), P(), P(), P(), P())
    out_specs = (P(None, "gx", "gy", None), P(None, ("gx", "gy")), P(), P(None, ("gx", "gy")), P())
    return jax.shard_map(
        on_device, mesh=mesh, in_specs=in_specs, out_specs=out_specs, check_vma=False
    )
```

```python
import functools

import jax
import jax.numpy as jnp
from jax import lax
from jax.experimental import pallas as pl
from jax.experimental.pallas import tpu as pltpu
from jax.sharding import PartitionSpec as P

CODE_LOW = -8.0
CODE_HIGH = 7.0
REPORT = 2.0 ** (-10)
WAYS = [(dx, dy) for dx in (-1, 0, 1) for dy in (-1, 0, 1) if (dx, dy) != (0, 0)]


def quantize(weight, scale):
    ratio = weight / scale
    level = jnp.clip(jnp.floor(ratio + 0.5), CODE_LOW, CODE_HIGH)
    inside = jnp.logical_and(ratio >= CODE_LOW, ratio <= CODE_HIGH)
    return level, inside, jnp.where(inside, level - ratio, level)


def halves(value):
    high = value.astype(jnp.bfloat16)
    low = (value - high.astype(jnp.float32)).astype(jnp.bfloat16)
    return high, low


def kernel(
    sizes, vol, cot, s1, s2, w1, w2, out, share1, share2,
    pad0, pad1, pad2, pad3, vol_h, hid_h, del_h, stage, slope,
    f1, f2, b2, b1, g1, g2, folded, box1, box2, land1, land2,
    send_sem, recv_sem, out_sem, in_sem,
):
    nx, ny, ch, width = vol.shape
    size_x, size_y = sizes
    me_x, me_y = lax.axis_index("gx"), lax.axis_index("gy")
    devices = size_x * size_y
    me = me_x * size_y + me_y
    group = devices // box1.shape[0]
    lane = lax.broadcasted_iota(jnp.int32, (ch, width), 1)

    for pad in (pad0, pad1, pad2, pad3):
        pad[...] = jnp.zeros_like(pad)

    def there(dx, dy):
        x, y = me_x + dx, me_y + dy
        return (x >= 0) & (x < size_x) & (y >= 0) & (y < size_y)

    barrier = pltpu.get_barrier_semaphore()

    def greet(k, carry):
        other = lax.rem(me + k, devices)
        pl.semaphore_signal(
            barrier, inc=1, device_id=(other // size_y, lax.rem(other, size_y)),
            device_id_type=pl.DeviceIdType.MESH,
        )
        return carry

    lax.fori_loop(1, devices, greet, 0)
    pad0[1:nx + 1, 1:ny + 1] = vol[...]
    pl.semaphore_wait(barrier, devices - 1)

    def spans(step, length):
        if step == 1:
            return pl.ds(length, 1), pl.ds(0, 1)
        if step == -1:
            return pl.ds(1, 1), pl.ds(length + 1, 1)
        return pl.ds(1, length), pl.ds(1, length)

    def remote(pad, turn, way, dx, dy):
        from_x, to_x = spans(dx, nx)
        from_y, to_y = spans(dy, ny)
        return pltpu.make_async_remote_copy(
            src_ref=pad.at[from_x, from_y],
            dst_ref=pad.at[to_x, to_y],
            send_sem=send_sem.at[turn, way],
            recv_sem=recv_sem.at[turn, way],
            device_id=(me_x + dx, me_y + dy),
            device_id_type=pl.DeviceIdType.MESH,
        )

    def send(pad, turn):
        for way, (dx, dy) in enumerate(WAYS):
            @pl.when(there(dx, dy))
            def _(way=way, dx=dx, dy=dy):
                remote(pad, turn, way, dx, dy).start()

    def receive(pad, turn):
        for way, (dx, dy) in enumerate(WAYS):
            @pl.when(there(-dx, -dy))
            def _(way=way, dx=dx, dy=dy):
                remote(pad, turn, way, dx, dy).wait_recv()

    def sent(pad, turn):
        for way, (dx, dy) in enumerate(WAYS):
            @pl.when(there(dx, dy))
            def _(way=way, dx=dx, dy=dy):
                remote(pad, turn, way, dx, dy).wait_send()

    def split(pad, target):
        for x in range(nx + 2):
            def body(y, carry, x=x):
                high, low = halves(pad[x, y])
                target[x, y, 0:ch, :] = high
                target[x, y, ch:2 * ch, :] = low
                return carry

            lax.fori_loop(0, ny + 2, body, 0)

    def doubled(weight, tap):
        value = weight[tap]
        return jnp.concatenate([value, value], axis=1)

    def tap_place(a, b, c):
        at = (3 * a + b) * 2 * ch
        return slice(c * ch, (c + 1) * ch), slice(at, at + 2 * ch)

    taps = [(a, b, c) for a in range(3) for b in range(3) for c in range(3)]

    def forward_matrix(weight, scale, forward):
        for tap, (a, b, c) in enumerate(taps):
            level, _, _ = quantize(doubled(weight, tap), scale[...])
            forward[tap_place(a, b, c)] = level.astype(jnp.bfloat16)

    def backward_matrix(forward, backward):
        low_lanes = lane < ch
        for first in range(0, 27, 2):
            some = taps[first:first + 2]
            values = [forward[tap_place(*tap)].astype(jnp.float32) for tap in some]
            mixed = jnp.where(low_lanes, values[0], values[-1])
            turned = jnp.concatenate([mixed, mixed], axis=0).T.astype(jnp.bfloat16)
            for k, (a, b, c) in enumerate(some):
                backward[tap_place(2 - a, 2 - b, 2 - c)] = turned[k * ch:(k + 1) * ch]

    def around(source, x, y):
        blocks = []
        for k in (0, 1):
            blocks.append(jnp.concatenate(
                [source[x + a, pl.ds(y + k, 3)].reshape(6 * ch, width) for a in range(3)],
                axis=0,
            ))
        return jnp.concatenate(blocks, axis=1)

    def conv_rows(source, matrix, x, y):
        total = jnp.dot(
            matrix[...], around(source, x, y), preferred_element_type=jnp.float32
        )
        rows = []
        for k in (0, 1):
            part = total[:, k * width:(k + 1) * width]
            before = jnp.where(lane == 0, 0.0, pltpu.roll(part[0:ch], 1, 1))
            after = jnp.where(
                lane == width - 1, 0.0, pltpu.roll(part[2 * ch:3 * ch], width - 1, 1)
            )
            rows.append(before + part[ch:2 * ch] + after)
        return rows

    def grad_rows(source, target, x, y):
        stacks = []
        for k in (0, 1):
            delta = stage[x, y + k]
            left = jnp.where(lane == width - 1, 0.0, pltpu.roll(delta, width - 1, 1))
            right = jnp.where(lane == 0, 0.0, pltpu.roll(delta, 1, 1))
            parts = []
            for shifted in (left, delta, right):
                parts.extend(halves(shifted))
            stacks.append(jnp.concatenate(parts, axis=0))
        prod = lax.dot_general(
            jnp.concatenate(stacks, axis=1), around(source, x, y),
            (((1,), (1,)), ((), ())), preferred_element_type=jnp.float32,
        )
        for c in range(3):
            first = prod[2 * c * ch:(2 * c + 1) * ch]
            second = prod[(2 * c + 1) * ch:(2 * c + 2) * ch]
            target[c * ch:(c + 1) * ch, :] += first + second

    def each_pair(body):
        pairs = ny // 2
        joined = 2 if pairs % 2 == 0 else 1
        for x in range(nx):
            def step(j, carry, x=x):
                for k in range(joined):
                    body(x, 2 * (j * joined + k))
                return carry

            lax.fori_loop(0, pairs // joined, step, 0)

    def collect(target, weight, scale, box):
        summed = jnp.zeros((ch, 2 * ch), jnp.float32)
        for a in range(3):
            for b in range(3):
                for c in range(3):
                    tap = 9 * a + 3 * b + c
                    at = (3 * a + b) * 2 * ch
                    value = target[c * ch:(c + 1) * ch, at:at + 2 * ch]
                    value = value + pltpu.roll(value, ch, 1)
                    _, inside, residue = quantize(doubled(weight, tap), scale[...])
                    summed = summed + value * residue
                    folded[tap] = jnp.where(inside, value, 0.0)
        line = 0.5 * jnp.sum(jnp.concatenate([summed, summed], axis=0).T, axis=0, keepdims=True)
        half = lax.broadcasted_iota(jnp.int32, (ch // 2, 2 * ch), 1) < ch
        for tap in range(27):
            even = folded[tap, pl.ds(0, ch // 2, stride=2), :]
            odd = folded[tap, pl.ds(1, ch // 2, stride=2), :]
            box[:, tap, :] = jnp.where(half, even, odd)
        box[:, 27, :] = jnp.broadcast_to(line, (ch // 2, 2 * ch))

    def scatter(box, land, turn):
        def one(k, carry):
            other = lax.rem(me + k, devices)
            pltpu.make_async_remote_copy(
                src_ref=box.at[other // group],
                dst_ref=land.at[k],
                send_sem=out_sem.at[turn],
                recv_sem=in_sem.at[turn],
                device_id=(other // size_y, lax.rem(other, size_y)),
                device_id_type=pl.DeviceIdType.MESH,
            ).start()
            return carry

        lax.fori_loop(1, devices, one, 0)
        land[0] = box[me // group]

    def gather(land, turn, share):
        others = land.at[pl.ds(1, devices - 1)]
        pltpu.make_async_copy(others, others, in_sem.at[turn]).wait()

        def add(source, total):
            return total + land[lax.rem(me - source + devices, devices)]

        share[...] = lax.fori_loop(0, devices, add, jnp.zeros(share.shape, jnp.float32))
        pltpu.make_async_copy(others, others, out_sem.at[turn]).wait()

    send(pad0, 0)
    forward_matrix(w1, s1, f1)
    forward_matrix(w2, s2, f2)
    g1[...] = jnp.zeros_like(g1)
    g2[...] = jnp.zeros_like(g2)
    box1[...] = jnp.zeros_like(box1)
    box2[...] = jnp.zeros_like(box2)
    receive(pad0, 0)
    split(pad0, vol_h)

    def first(x, y):
        for k, row in enumerate(conv_rows(vol_h, f1, x, y)):
            pre = row * s1[...]
            sig = 1.0 / (1.0 + jnp.exp(-pre))
            stage[x, y + k] = pre * sig
            slope[x, y + k] = sig * (1.0 + pre * (1.0 - sig))

    each_pair(first)

    pad1[1:nx + 1, 1:ny + 1] = stage[...]
    send(pad1, 1)
    backward_matrix(f2, b2)
    backward_matrix(f1, b1)
    receive(pad1, 1)
    split(pad1, hid_h)

    def second(x, y):
        for k, row in enumerate(conv_rows(hid_h, f2, x, y)):
            pre = row * s2[...]
            sig = 1.0 / (1.0 + jnp.exp(-pre))
            stage[x, y + k] = cot[x, y + k] * (sig * (1.0 + pre * (1.0 - sig)))

    each_pair(second)

    pad2[1:nx + 1, 1:ny + 1] = stage[...] * s2[...]
    send(pad2, 2)
    each_pair(lambda x, y: grad_rows(hid_h, g2, x, y))
    collect(g2, w2, s2, box2)
    scatter(box2, land2, 1)
    receive(pad2, 2)
    split(pad2, del_h)

    def third(x, y):
        for k, row in enumerate(conv_rows(del_h, b2, x, y)):
            stage[x, y + k] = row * slope[x, y + k]

    each_pair(third)

    pad3[1:nx + 1, 1:ny + 1] = stage[...] * s1[...]
    send(pad3, 3)
    each_pair(lambda x, y: grad_rows(vol_h, g1, x, y))
    collect(g1, w1, s1, box1)
    scatter(box1, land1, 0)
    receive(pad3, 3)
    split(pad3, del_h)

    def fourth(x, y):
        for k, row in enumerate(conv_rows(del_h, b1, x, y)):
            out[x, y + k] = row

    each_pair(fourth)
    gather(land2, 1, share2)
    gather(land1, 0, share1)
    for turn, pad in enumerate((pad0, pad1, pad2, pad3)):
        sent(pad, turn)


def on_device(volume, cotangent, weight_one, scale_one, weight_two, scale_two):
    channels = scale_one.shape[0]
    ch, nx, ny, width = volume.shape
    sizes = (lax.axis_size("gx"), lax.axis_size("gy"))
    devices = sizes[0] * sizes[1]
    vmem = pl.BlockSpec(memory_space=pltpu.VMEM)
    cells = jax.ShapeDtypeStruct((nx, ny, ch, width), jnp.float32)
    block = jax.ShapeDtypeStruct((32, 2 * ch), jnp.float32)
    pad = pltpu.VMEM((nx + 2, ny + 2, ch, width), jnp.float32)
    half = pltpu.VMEM((nx + 2, ny + 2, 2 * ch, width), jnp.bfloat16)
    local = pltpu.VMEM((nx, ny, ch, width), jnp.float32)
    matrix = pltpu.VMEM((3 * ch, 18 * ch), jnp.bfloat16)
    grads = pltpu.VMEM((3 * ch, 18 * ch), jnp.float32)
    box = pltpu.VMEM((ch // 2, 32, 2 * ch), jnp.float32)
    land = pltpu.VMEM((devices, 32, 2 * ch), jnp.float32)

    moved, block_one, block_two = pl.pallas_call(
        functools.partial(kernel, sizes),
        out_shape=(cells, block, block),
        in_specs=[vmem] * 6,
        out_specs=(vmem, vmem, vmem),
        scratch_shapes=[
            pad, pad, pad, pad, half, half, half, local, local,
            matrix, matrix, matrix, matrix, grads, grads,
            pltpu.VMEM((27, ch, 2 * ch), jnp.float32), box, box, land, land,
            pltpu.SemaphoreType.DMA((4, 8)),
            pltpu.SemaphoreType.DMA((4, 8)),
            pltpu.SemaphoreType.DMA((2,)),
            pltpu.SemaphoreType.DMA((2,)),
        ],
        compiler_params=pltpu.CompilerParams(
            collective_id=0, has_side_effects=True, vmem_limit_bytes=52 * 2 ** 20
        ),
    )(
        volume.transpose(1, 2, 0, 3),
        cotangent.transpose(1, 2, 0, 3),
        jnp.broadcast_to(scale_one[:, None], (ch, width)),
        jnp.broadcast_to(scale_two[:, None], (ch, width)),
        weight_one.reshape(27, ch, ch),
        weight_two.reshape(27, ch, ch),
    )
    input_grad = moved.transpose(2, 0, 1, 3)
    share = channels * channels // devices
    group = 2 * ch // share
    first_col = lax.rem(lax.axis_index(("gx", "gy")), group) * share
    factor = REPORT * (27.0 * channels * CODE_HIGH) ** (-0.5)

    def results(block):
        kernels = lax.dynamic_slice(block, (0, first_col), (27, share)) * REPORT
        return kernels, block[27, :channels] * factor

    kernel_one, scales_one = results(block_one)
    kernel_two, scales_two = results(block_two)
    return (input_grad, kernel_one, scales_one, kernel_two, scales_two)


def solution(mesh):
    in_specs = (P(None, "gx", "gy", None), P(None, "gx", "gy", None), P(), P(), P(), P())
    out_specs = (P(None, "gx", "gy", None), P(None, ("gx", "gy")), P(), P(None, ("gx", "gy")), P())
    return jax.shard_map(
        on_device, mesh=mesh, in_specs=in_specs, out_specs=out_specs, check_vma=False
    )
```

```python
import functools

import jax
import jax.numpy as jnp
from jax import lax
from jax.experimental import pallas as pl
from jax.experimental.pallas import tpu as pltpu
from jax.sharding import PartitionSpec as P

CODE_LOW = -8.0
CODE_HIGH = 7.0
REPORT = 2.0 ** (-10)
WAYS = [(dx, dy) for dx in (-1, 0, 1) for dy in (-1, 0, 1) if (dx, dy) != (0, 0)]


def quantize(weight, scale):
    ratio = weight / scale
    level = jnp.clip(jnp.floor(ratio + 0.5), CODE_LOW, CODE_HIGH)
    inside = jnp.logical_and(ratio >= CODE_LOW, ratio <= CODE_HIGH)
    return level, inside, jnp.where(inside, level - ratio, level)


def halves(value):
    high = value.astype(jnp.bfloat16)
    low = (value - high.astype(jnp.float32)).astype(jnp.bfloat16)
    return high, low


def kernel(
    sizes, vol, cot, s1, s2, w1, w2, out, share1, share2,
    pad0, pad1, pad2, pad3, vol_h, hid_h, del_h, stage, slope,
    f1, f2, b2, b1, g1, g2, folded, box1, box2, land1, land2,
    swap1, swap2, merged1, merged2,
    send_sem, recv_sem, out_sem, in_sem, pass_sem, take_sem,
):
    nx, ny, ch, width = vol.shape
    size_x, size_y = sizes
    me_x, me_y = lax.axis_index("gx"), lax.axis_index("gy")
    devices = size_x * size_y
    me = me_x * size_y + me_y
    chips = devices // 2
    core = lax.rem(me, 2)
    chip = me // 2
    sets, boxes = box1.shape[0], box1.shape[1]
    owners = devices // boxes
    lane = lax.broadcasted_iota(jnp.int32, (ch, width), 1)

    for pad in (pad0, pad1, pad2, pad3):
        pad[...] = jnp.zeros_like(pad)

    def there(dx, dy):
        x, y = me_x + dx, me_y + dy
        return (x >= 0) & (x < size_x) & (y >= 0) & (y < size_y)

    barrier = pltpu.get_barrier_semaphore()

    def greet(k, carry):
        other = lax.rem(me + k, devices)
        pl.semaphore_signal(
            barrier, inc=1, device_id=(other // size_y, lax.rem(other, size_y)),
            device_id_type=pl.DeviceIdType.MESH,
        )
        return carry

    lax.fori_loop(1, devices, greet, 0)
    pad0[1:nx + 1, 1:ny + 1] = vol[...]
    pl.semaphore_wait(barrier, devices - 1)

    def spans(step, length):
        if step == 1:
            return pl.ds(length, 1), pl.ds(0, 1)
        if step == -1:
            return pl.ds(1, 1), pl.ds(length + 1, 1)
        return pl.ds(1, length), pl.ds(1, length)

    def remote(pad, turn, way, dx, dy):
        from_x, to_x = spans(dx, nx)
        from_y, to_y = spans(dy, ny)
        return pltpu.make_async_remote_copy(
            src_ref=pad.at[from_x, from_y],
            dst_ref=pad.at[to_x, to_y],
            send_sem=send_sem.at[turn, way],
            recv_sem=recv_sem.at[turn, way],
            device_id=(me_x + dx, me_y + dy),
            device_id_type=pl.DeviceIdType.MESH,
        )

    def send(pad, turn):
        for way, (dx, dy) in enumerate(WAYS):
            @pl.when(there(dx, dy))
            def _(way=way, dx=dx, dy=dy):
                remote(pad, turn, way, dx, dy).start()

    def receive(pad, turn):
        for way, (dx, dy) in enumerate(WAYS):
            @pl.when(there(-dx, -dy))
            def _(way=way, dx=dx, dy=dy):
                remote(pad, turn, way, dx, dy).wait_recv()

    def sent(pad, turn):
        for way, (dx, dy) in enumerate(WAYS):
            @pl.when(there(dx, dy))
            def _(way=way, dx=dx, dy=dy):
                remote(pad, turn, way, dx, dy).wait_send()

    def split(pad, target):
        for x in range(nx + 2):
            def body(y, carry, x=x):
                high, low = halves(pad[x, y])
                target[x, y, 0:ch, :] = high
                target[x, y, ch:2 * ch, :] = low
                return carry

            lax.fori_loop(0, ny + 2, body, 0)

    def doubled(weight, tap):
        value = weight[tap]
        return jnp.concatenate([value, value], axis=1)

    def tap_place(a, b, c):
        at = (3 * a + b) * 2 * ch
        return slice(c * ch, (c + 1) * ch), slice(at, at + 2 * ch)

    taps = [(a, b, c) for a in range(3) for b in range(3) for c in range(3)]

    def forward_matrix(weight, scale, forward):
        for tap, (a, b, c) in enumerate(taps):
            level, _, _ = quantize(doubled(weight, tap), scale[...])
            forward[tap_place(a, b, c)] = level.astype(jnp.bfloat16)

    def backward_matrix(forward, backward):
        low_lanes = lane < ch
        for first in range(0, 27, 2):
            some = taps[first:first + 2]
            values = [forward[tap_place(*tap)].astype(jnp.float32) for tap in some]
            mixed = jnp.where(low_lanes, values[0], values[-1])
            turned = jnp.concatenate([mixed, mixed], axis=0).T.astype(jnp.bfloat16)
            for k, (a, b, c) in enumerate(some):
                backward[tap_place(2 - a, 2 - b, 2 - c)] = turned[k * ch:(k + 1) * ch]

    def around(source, x, y):
        blocks = []
        for k in (0, 1):
            blocks.append(jnp.concatenate(
                [source[x + a, pl.ds(y + k, 3)].reshape(6 * ch, width) for a in range(3)],
                axis=0,
            ))
        return jnp.concatenate(blocks, axis=1)

    def conv_rows(source, matrix, x, y):
        total = jnp.dot(
            matrix[...], around(source, x, y), preferred_element_type=jnp.float32
        )
        rows = []
        for k in (0, 1):
            part = total[:, k * width:(k + 1) * width]
            before = jnp.where(lane == 0, 0.0, pltpu.roll(part[0:ch], 1, 1))
            after = jnp.where(
                lane == width - 1, 0.0, pltpu.roll(part[2 * ch:3 * ch], width - 1, 1)
            )
            rows.append(before + part[ch:2 * ch] + after)
        return rows

    def grad_rows(source, target, x, y):
        stacks = []
        for k in (0, 1):
            delta = stage[x, y + k]
            left = jnp.where(lane == width - 1, 0.0, pltpu.roll(delta, width - 1, 1))
            right = jnp.where(lane == 0, 0.0, pltpu.roll(delta, 1, 1))
            parts = []
            for shifted in (left, delta, right):
                parts.extend(halves(shifted))
            stacks.append(jnp.concatenate(parts, axis=0))
        prod = lax.dot_general(
            jnp.concatenate(stacks, axis=1), around(source, x, y),
            (((1,), (1,)), ((), ())), preferred_element_type=jnp.float32,
        )
        for c in range(3):
            first = prod[2 * c * ch:(2 * c + 1) * ch]
            second = prod[(2 * c + 1) * ch:(2 * c + 2) * ch]
            target[c * ch:(c + 1) * ch, :] += first + second

    def each_pair(body):
        pairs = ny // 2
        joined = 2 if pairs % 2 == 0 else 1
        for x in range(nx):
            def step(j, carry, x=x):
                for k in range(joined):
                    body(x, 2 * (j * joined + k))
                return carry

            lax.fori_loop(0, pairs // joined, step, 0)

    def collect(target, weight, scale, box):
        summed = jnp.zeros((ch, 2 * ch), jnp.float32)
        for a in range(3):
            for b in range(3):
                for c in range(3):
                    tap = 9 * a + 3 * b + c
                    at = (3 * a + b) * 2 * ch
                    value = target[c * ch:(c + 1) * ch, at:at + 2 * ch]
                    value = value + pltpu.roll(value, ch, 1)
                    _, inside, residue = quantize(doubled(weight, tap), scale[...])
                    summed = summed + value * residue
                    folded[tap] = jnp.where(inside, value, 0.0)
        line = 0.5 * jnp.sum(jnp.concatenate([summed, summed], axis=0).T, axis=0, keepdims=True)
        half = lax.broadcasted_iota(jnp.int32, (boxes, 2 * ch), 1) < ch
        for k in range(sets):
            for tap in range(27):
                even = folded[tap, pl.ds(2 * k, boxes, stride=2 * sets), :]
                odd = folded[tap, pl.ds(2 * k + 1, boxes, stride=2 * sets), :]
                box[k, :, tap, :] = jnp.where(half, even, odd)
            box[k, :, 27, :] = jnp.broadcast_to(line, (boxes, 2 * ch))

    def exchange(box, swap, turn):
        return pltpu.make_async_remote_copy(
            src_ref=box.at[lax.rem(1 - core, sets)],
            dst_ref=swap,
            send_sem=pass_sem.at[turn],
            recv_sem=take_sem.at[turn],
            device_id=(me_x, me_y + 1 - 2 * core),
            device_id_type=pl.DeviceIdType.MESH,
        )

    def scatter(box, swap, merged, land, turn):
        exchange(box, swap, turn).wait_recv()
        merged[...] = box[lax.rem(core, sets)] + swap[...]

        def one(k, carry):
            other = 2 * lax.rem(chip + k, chips) + core
            pltpu.make_async_remote_copy(
                src_ref=merged.at[other // owners],
                dst_ref=land.at[k],
                send_sem=out_sem.at[turn],
                recv_sem=in_sem.at[turn],
                device_id=(other // size_y, lax.rem(other, size_y)),
                device_id_type=pl.DeviceIdType.MESH,
            ).start()
            return carry

        lax.fori_loop(1, chips, one, 0)
        land[0] = merged[me // owners]

    def gather(land, turn, share):
        others = land.at[pl.ds(1, chips - 1)]
        pltpu.make_async_copy(others, others, in_sem.at[turn]).wait()

        def add(source, total):
            return total + land[lax.rem(chip - source + chips, chips)]

        share[...] = lax.fori_loop(0, chips, add, jnp.zeros(share.shape, jnp.float32))
        pltpu.make_async_copy(others, others, out_sem.at[turn]).wait()

    send(pad0, 0)
    forward_matrix(w1, s1, f1)
    forward_matrix(w2, s2, f2)
    g1[...] = jnp.zeros_like(g1)
    g2[...] = jnp.zeros_like(g2)
    box1[...] = jnp.zeros_like(box1)
    box2[...] = jnp.zeros_like(box2)
    receive(pad0, 0)
    split(pad0, vol_h)

    def first(x, y):
        for k, row in enumerate(conv_rows(vol_h, f1, x, y)):
            pre = row * s1[...]
            sig = 1.0 / (1.0 + jnp.exp(-pre))
            stage[x, y + k] = pre * sig
            slope[x, y + k] = sig * (1.0 + pre * (1.0 - sig))

    each_pair(first)

    pad1[1:nx + 1, 1:ny + 1] = stage[...]
    send(pad1, 1)
    backward_matrix(f2, b2)
    backward_matrix(f1, b1)
    receive(pad1, 1)
    split(pad1, hid_h)

    def second(x, y):
        for k, row in enumerate(conv_rows(hid_h, f2, x, y)):
            pre = row * s2[...]
            sig = 1.0 / (1.0 + jnp.exp(-pre))
            stage[x, y + k] = cot[x, y + k] * (sig * (1.0 + pre * (1.0 - sig)))

    each_pair(second)

    pad2[1:nx + 1, 1:ny + 1] = stage[...] * s2[...]
    send(pad2, 2)
    each_pair(lambda x, y: grad_rows(hid_h, g2, x, y))
    collect(g2, w2, s2, box2)
    exchange(box2, swap2, 1).start()
    receive(pad2, 2)
    split(pad2, del_h)
    scatter(box2, swap2, merged2, land2, 1)

    def third(x, y):
        for k, row in enumerate(conv_rows(del_h, b2, x, y)):
            stage[x, y + k] = row * slope[x, y + k]

    each_pair(third)

    pad3[1:nx + 1, 1:ny + 1] = stage[...] * s1[...]
    send(pad3, 3)
    each_pair(lambda x, y: grad_rows(vol_h, g1, x, y))
    collect(g1, w1, s1, box1)
    exchange(box1, swap1, 0).start()
    receive(pad3, 3)
    split(pad3, del_h)
    scatter(box1, swap1, merged1, land1, 0)

    def fourth(x, y):
        for k, row in enumerate(conv_rows(del_h, b1, x, y)):
            out[x, y + k] = row

    each_pair(fourth)
    gather(land2, 1, share2)
    gather(land1, 0, share1)
    for turn, pad in enumerate((pad0, pad1, pad2, pad3)):
        sent(pad, turn)
    exchange(box1, swap1, 0).wait_send()
    exchange(box2, swap2, 1).wait_send()


def on_device(volume, cotangent, weight_one, scale_one, weight_two, scale_two):
    channels = scale_one.shape[0]
    ch, nx, ny, width = volume.shape
    sizes = (lax.axis_size("gx"), lax.axis_size("gy"))
    devices = sizes[0] * sizes[1]
    vmem = pl.BlockSpec(memory_space=pltpu.VMEM)
    cells = jax.ShapeDtypeStruct((nx, ny, ch, width), jnp.float32)
    block = jax.ShapeDtypeStruct((32, 2 * ch), jnp.float32)
    pad = pltpu.VMEM((nx + 2, ny + 2, ch, width), jnp.float32)
    half = pltpu.VMEM((nx + 2, ny + 2, 2 * ch, width), jnp.bfloat16)
    local = pltpu.VMEM((nx, ny, ch, width), jnp.float32)
    matrix = pltpu.VMEM((3 * ch, 18 * ch), jnp.bfloat16)
    grads = pltpu.VMEM((3 * ch, 18 * ch), jnp.float32)
    sets = 2 if devices == ch // 2 else 1
    boxes = ch // 2 // sets
    box = pltpu.VMEM((sets, boxes, 32, 2 * ch), jnp.float32)
    part = pltpu.VMEM((boxes, 32, 2 * ch), jnp.float32)
    land = pltpu.VMEM((devices // 2, 32, 2 * ch), jnp.float32)

    moved, block_one, block_two = pl.pallas_call(
        functools.partial(kernel, sizes),
        out_shape=(cells, block, block),
        in_specs=[vmem] * 6,
        out_specs=(vmem, vmem, vmem),
        scratch_shapes=[
            pad, pad, pad, pad, half, half, half, local, local,
            matrix, matrix, matrix, matrix, grads, grads,
            pltpu.VMEM((27, ch, 2 * ch), jnp.float32), box, box, land, land,
            part, part, part, part,
            pltpu.SemaphoreType.DMA((4, 8)),
            pltpu.SemaphoreType.DMA((4, 8)),
            pltpu.SemaphoreType.DMA((2,)),
            pltpu.SemaphoreType.DMA((2,)),
            pltpu.SemaphoreType.DMA((2,)),
            pltpu.SemaphoreType.DMA((2,)),
        ],
        compiler_params=pltpu.CompilerParams(
            collective_id=0, has_side_effects=True, vmem_limit_bytes=52 * 2 ** 20
        ),
    )(
        volume.transpose(1, 2, 0, 3),
        cotangent.transpose(1, 2, 0, 3),
        jnp.broadcast_to(scale_one[:, None], (ch, width)),
        jnp.broadcast_to(scale_two[:, None], (ch, width)),
        weight_one.reshape(27, ch, ch),
        weight_two.reshape(27, ch, ch),
    )
    input_grad = moved.transpose(2, 0, 1, 3)
    share = channels * channels // devices
    group = 2 * ch // share
    first_col = lax.rem(lax.axis_index(("gx", "gy")), group) * share
    factor = REPORT * (27.0 * channels * CODE_HIGH) ** (-0.5)

    def results(block):
        kernels = lax.dynamic_slice(block, (0, first_col), (27, share)) * REPORT
        return kernels, block[27, :channels] * factor

    kernel_one, scales_one = results(block_one)
    kernel_two, scales_two = results(block_two)
    return (input_grad, kernel_one, scales_one, kernel_two, scales_two)


def solution(mesh):
    in_specs = (P(None, "gx", "gy", None), P(None, "gx", "gy", None), P(), P(), P(), P())
    out_specs = (P(None, "gx", "gy", None), P(None, ("gx", "gy")), P(), P(None, ("gx", "gy")), P())
    return jax.shard_map(
        on_device, mesh=mesh, in_specs=in_specs, out_specs=out_specs, check_vma=False
    )
```
